256 devices in a mesh: ctx: 32 (over z, y_lo, core), tp: 8 (over x, y_hi).
Axes of the slice: x: 4, y: 4 (y_hi: 2, y_lo: 2; y = y_hi * 2 + y_lo), z: 8, core: 2. Of those that a mesh axis runs over, the one named last changes fastest.
Arguments:
- queries: bfloat16 [4096, 64, 128], P('ctx', 'tp'), may hold values from -5 to 5
- key_states: bfloat16 [4096, 8, 128], P('ctx', 'tp'), may hold values from -5 to 5
- value_vectors: bfloat16 [4096, 8, 128], P('ctx', 'tp'), may hold values from -6 to 6
- grad_output: bfloat16 [4096, 8192], P(('ctx', 'tp')), may hold values from -6 to 6
- out_weight: bfloat16 [8192, 8192], P('ctx', 'tp'), may hold values from -0.0625 to 0.0625
- doc_lengths: int32 [8], replicated, may hold values from 1 to 2560, as said below
Outputs:
- query_grads: bfloat16 [4096, 64, 128], P('ctx', 'tp')
- key_gradient: bfloat16 [4096, 8, 128], P('ctx', 'tp')
- value_gradient: bfloat16 [4096, 8, 128], P('ctx', 'tp')
The draws below stay inside these ranges and needn't reach their ends.
Inputs may be any that keep to these rules, and one draw needn't show every extreme that they name: `doc_lengths`: the lengths sum to 4096; exactly one document is 2560 positions long, every other one is shorter.
All inputs are finite; a program needn't handle non-finite values.
Results may differ from the reference program's by a relative error of at most 0.02.
Values may be sent and summed in bfloat16 or wider, within the bound.
No kernel may reach another device: no remote copies, remote signals or barrier semaphores. Data moves between devices by JAX's collectives and lax.ppermute only.
A program may use at most 64 MiB of HBM per device.

```python
import jax
import jax.numpy as jnp
from jax import lax

D = 8192
QUERY_HEADS = 64
KEY_VALUE_HEADS = 8
HEAD_SIZE = 128
DOCS = 8
TOKEN_COUNT = 4096


def document_lengths(key):
    weights = jax.random.randint(jax.random.fold_in(key, 11), (DOCS,), 1, 8)
    largest = jax.random.randint(jax.random.fold_in(key, 12), (), 0, DOCS)
    longest = TOKEN_COUNT * 5 // 8
    remainder = TOKEN_COUNT - longest
    doc_index = jnp.arange(DOCS, dtype=jnp.int32)
    others = jnp.where(doc_index == largest, 0, weights)
    portion = others * remainder // jnp.sum(others)
    leftover = remainder - jnp.sum(portion)
    portion = portion + jnp.where(doc_index == (largest + 1) % DOCS, leftover, 0)
    return jnp.where(doc_index == largest, longest, portion).astype(jnp.int32)


def draw_doc_lengths(key, part):
    lengths = document_lengths(key)
    return lengths


def draw_queries(key, part):
    key = jax.random.fold_in(key, 2)
    current_values = jnp.clip(jax.random.normal(key, (TOKEN_COUNT, QUERY_HEADS, HEAD_SIZE), jnp.float32), -5.0, 5.0)
    return current_values.astype(jnp.bfloat16)


def draw_key_states(key, part):
    key = jax.random.fold_in(key, 3)
    current_values = jnp.clip(jax.random.normal(key, (TOKEN_COUNT, KEY_VALUE_HEADS, HEAD_SIZE), jnp.float32), -5.0, 5.0)
    return current_values.astype(jnp.bfloat16)


def levels(own_key, shape, cuts, low, high):
    loudness, own = 1.0, jax.random.fold_in(own_key, 6)
    for dim, shards_of in cuts:
        draws = jnp.exp(jax.random.uniform(jax.random.fold_in(own, dim), (shards_of,), jnp.float32, low / len(cuts), high / len(cuts)))
        loudness = loudness * jnp.repeat(draws, shape[dim] // shards_of).reshape([-1 if axis == dim else 1 for axis in range(len(shape))])
    return loudness


def centred(key, shape, scale, reach, cuts=(), kind=jnp.bfloat16):
    gain = levels(key, shape, cuts, -0.22, 0.18) if cuts else 1.0
    drawn = jax.random.normal(key, shape, jnp.float32) * scale * gain
    return jnp.minimum(jnp.maximum(drawn, -reach), reach).astype(kind)


def setup_inputs(seed: int = 0) -> dict:
    key_list = jax.random.split(jax.random.key(seed), 7)
    return {
        "queries": draw_queries(jax.random.fold_in(key_list[6], 71), 0),
        "key_states": draw_key_states(jax.random.fold_in(key_list[6], 71), 0),
        "value_vectors": centred(key_list[2], (TOKEN_COUNT, KEY_VALUE_HEADS, HEAD_SIZE), 1.0, 6.0, ((0, 32), (1, 8))),
        "grad_output": centred(key_list[3], (TOKEN_COUNT, D), 1.0, 6.0, ((0, 256),)),
        "out_weight": centred(key_list[4], (D, QUERY_HEADS * HEAD_SIZE), D ** -0.5, 0.0625, ((0, 32), (1, 8))),
        "doc_lengths": draw_doc_lengths(jax.random.fold_in(key_list[6], 71), 0),
    }


def doc_of(doc_ends, position):
    return jnp.sum((doc_ends[None, :] <= position[:, None]).astype(jnp.int32), axis=1)


def reference(queries, key_states, value_vectors, grad_output, out_weight, doc_lengths):
    group_width = QUERY_HEADS // KEY_VALUE_HEADS
    score_scale = HEAD_SIZE ** -0.5
    highest = lax.Precision.HIGHEST
    position = jnp.arange(TOKEN_COUNT, dtype=jnp.int32)
    doc_ids = doc_of(jnp.cumsum(doc_lengths), position)
    allowed = (doc_ids[:, None] == doc_ids[None, :]) & (position[None, :] <= position[:, None])
    out_grad = jnp.dot(grad_output, out_weight, preferred_element_type=jnp.float32).astype(jnp.bfloat16)
    out_grad = out_grad.reshape(TOKEN_COUNT, QUERY_HEADS, HEAD_SIZE)

    def one_head(inputs):
        query_head = inputs[0].astype(jnp.float32)
        key_head = inputs[1].astype(jnp.float32)
        value_head = inputs[2].astype(jnp.float32)
        grad_head = inputs[3].astype(jnp.float32)
        scores = jnp.dot(query_head, key_head.T, precision=highest) * score_scale
        scores = jnp.where(allowed, scores, -jnp.inf)
        row_top = jnp.max(scores, axis=1, keepdims=True)
        log_total = row_top + jnp.log(jnp.sum(jnp.exp(scores - row_top), axis=1, keepdims=True))
        prob_tile = jnp.exp(scores - log_total)
        attention = jnp.dot(prob_tile, value_head, precision=highest)
        row_delta = jnp.sum(grad_head * attention, axis=1, keepdims=True)
        prob_low = lax.optimization_barrier(prob_tile.astype(jnp.bfloat16)).astype(jnp.float32)
        value_portion = jnp.dot(prob_low.T, grad_head, precision=highest)
        prob_grads = jnp.dot(grad_head, value_head.T, precision=highest)
        score_grads = (prob_tile * (prob_grads - row_delta)).astype(jnp.bfloat16)
        score_grads = lax.optimization_barrier(score_grads).astype(jnp.float32)
        query_part = jnp.dot(score_grads, key_head, precision=highest) * score_scale
        key_portion = jnp.dot(score_grads.T, query_head, precision=highest) * score_scale
        return query_part, key_portion, value_portion

    key_heads = jnp.repeat(key_states, group_width, axis=1).transpose(1, 0, 2)
    value_heads = jnp.repeat(value_vectors, group_width, axis=1).transpose(1, 0, 2)
    query_part, key_portion, value_portion = lax.map(
        one_head, (queries.transpose(1, 0, 2), key_heads, value_heads, out_grad.transpose(1, 0, 2)))
    query_grads = query_part.transpose(1, 0, 2).astype(jnp.bfloat16)
    key_gradient = jnp.sum(key_portion.reshape(KEY_VALUE_HEADS, group_width, TOKEN_COUNT, HEAD_SIZE), axis=1).transpose(1, 0, 2)
    value_gradient = jnp.sum(value_portion.reshape(KEY_VALUE_HEADS, group_width, TOKEN_COUNT, HEAD_SIZE), axis=1).transpose(1, 0, 2)
    return query_grads, key_gradient.astype(jnp.bfloat16), value_gradient.astype(jnp.bfloat16)
```

```python
import math

import jax
import jax.numpy as jnp
from jax import lax
from jax.experimental import pallas as pl
from jax.experimental.pallas import tpu as pltpu
from jax.sharding import Mesh, PartitionSpec as P

BF = jnp.bfloat16
F32 = jnp.float32
NEG = -1e30
HD = 128
SCALE = HD**-0.5
C2 = SCALE * math.log2(math.e)
PLANE = 512
PLANES = 6
ROWS = 1024
CHUNK = 256
VMEM = 58 * 1024 * 1024

NT = (((1,), (1,)), ((), ()))
NN = (((1,), (0,)), ((), ()))
TN = (((0,), (0,)), ((), ()))


def dot(a, b, dims):
    return lax.dot_general(a, b, dims, preferred_element_type=F32)


def key_positions(z, d):
    r = lax.broadcasted_iota(jnp.int32, (PLANE, 1), 0)
    part = r >> 7
    block = ((part & 1) << 1) | (part >> 1)
    return (z - d) * PLANE + block * 128 + (r & 127)


def project_kernel(s_ref, gh, gu, gd, gu2, gd2, w0, w1, w2, w3, w4, w5, w6, w7, send, keep, a_scr):
    me = s_ref[0]
    for rel in range(4):
        src = pl.multiple_of((me ^ rel) * 16, 16)
        for half in range(2):
            base = pl.multiple_of(src + half * 64, 16)
            for relx, ref, at in (
                (0, gh, base),
                (1, gd, base),
                (2, (gu2, gd2)[half], src),
                (3, gu, base),
            ):
                row = rel * 128 + (relx * 2 + half) * 16
                a_scr[row : row + 16, :] = ref[pl.ds(at, 16), :]
    ws = (w0, w1, w2, w3, w4, w5, w6, w7)
    for n in range(4):
        cols = slice(n * 256, n * 256 + 256)
        total = None
        for k in range(8):
            part = dot(a_scr[:, k * 256 : k * 256 + 256], ws[k][:, cols], NN)
            total = part if total is None else total + part
        keep[0, :, cols] = total[0:128]
        send[0, :, cols] = total[128:256].astype(BF)
        keep[1, :, cols] = total[256:384]
        send[1, :, cols] = total[384:512].astype(BF)


def forward_kernel(s_ref, q, kv, start, att, lse, m_scr, l_scr):
    z, count, pos0 = s_ref[0], s_ref[1], s_ref[2]
    m_scr[...] = jnp.full((1, ROWS), NEG, F32)
    l_scr[...] = jnp.zeros((1, ROWS), F32)
    att[...] = jnp.zeros((HD, ROWS), F32)

    def plane(d, carry):
        keys = key_positions(z, d)
        k = kv[d, :, 0:HD]
        v = kv[d, :, HD : 2 * HD]
        for n in range(ROWS // CHUNK):
            cols = slice(n * CHUNK, n * CHUNK + CHUNK)
            row_pos = pos0 + (lax.broadcasted_iota(jnp.int32, (1, CHUNK), 1) & 127)
            s = dot(k, q[cols, :], NT) * C2
            ok = (keys >= start[:, cols]) & (keys <= row_pos)
            s = jnp.where(ok, s, NEG)
            old = m_scr[:, cols]
            new = jnp.maximum(old, jnp.max(s, axis=0, keepdims=True))
            shrink = jnp.exp2(old - new)
            p = jnp.exp2(s - new)
            l_scr[:, cols] = l_scr[:, cols] * shrink + jnp.sum(p, axis=0, keepdims=True)
            m_scr[:, cols] = new
            att[:, cols] = att[:, cols] * shrink + dot(v, p.astype(BF), TN)
        return carry

    lax.fori_loop(0, count, plane, 0)
    lse[...] = m_scr[...] + jnp.log2(l_scr[...])
    att[...] = att[...] / l_scr[...]


def backward_kernel(
    s_ref, q, o, att, lse, kv, start, dq, keep, send, do_scr, delta, dq_scr, dk_scr, dv_scr
):
    z, count, pos0, c, x, yh = (s_ref[i] for i in range(6))
    for rel in range(8):
        tp = ((x + rel // 2) & 3) * 2 + (yh ^ (rel & 1))
        for h in range(8):
            at = pl.multiple_of(h * 128 + tp * 16, 16)
            do_scr[pl.ds(at, 16), :] = o[rel * 16 : rel * 16 + 16, h * HD : h * HD + HD]
    for h in range(8):
        cols = slice(h * 128, h * 128 + 128)
        do_t = do_scr[cols, :].astype(F32).T
        delta[:, cols] = jnp.sum(do_t * att[:, cols], axis=0, keepdims=True)
    dq_scr[...] = jnp.zeros((HD, ROWS), F32)

    def store(d, value):
        group = jnp.where((d >= 1) & (d <= 3), 0, 1)
        slot = jnp.where(d == 0, 2, jnp.where(d <= 3, d - 1, d - 4))

        @pl.when(group == c)
        def _():
            keep[slot] = value()

        @pl.when(group != c)
        def _():
            send[slot] = value()

    def plane(d, carry):
        keys = key_positions(z, d)
        k = kv[d, :, 0:HD]
        v = kv[d, :, HD : 2 * HD]
        k_t = k.astype(F32).T.astype(BF)
        for n in range(ROWS // CHUNK):
            cols = slice(n * CHUNK, n * CHUNK + CHUNK)
            row_pos = pos0 + (lax.broadcasted_iota(jnp.int32, (1, CHUNK), 1) & 127)
            qn = q[cols, :]
            don = do_scr[cols, :]
            s = dot(k, qn, NT) * C2 - lse[:, cols]
            ok = (keys >= start[:, cols]) & (keys <= row_pos)
            p = jnp.where(ok, jnp.exp2(s), 0.0)
            dv = dot(p.astype(BF), don, NN)
            dp = dot(v, don, NT)
            ds = (p * (dp - delta[:, cols])).astype(BF)
            dk = dot(ds, qn, NN)
            dq_scr[:, cols] += dot(k_t, ds, NN)
            if n == 0:
                dk_scr[...] = dk
                dv_scr[...] = dv
            else:
                dk_scr[...] += dk
                dv_scr[...] += dv
        store(d, lambda: jnp.concatenate([dk_scr[...] * SCALE, dv_scr[...]], axis=1).astype(BF))
        return carry

    lax.fori_loop(0, count, plane, 0)

    def blank(d, carry):
        store(d, lambda: jnp.zeros((PLANE, 2 * HD), BF))
        return carry

    lax.fori_loop(count, PLANES, blank, 0)
    for h in range(8):
        cols = slice(h * 128, h * 128 + 128)
        dq[:, cols] = (dq_scr[:, cols] * SCALE).T.astype(BF)


def in_vmem(n):
    return [pl.BlockSpec(memory_space=pltpu.SMEM)] + [pl.BlockSpec(memory_space=pltpu.VMEM)] * n


def call(kernel, n_in, outs, scratch, flops):
    return pl.pallas_call(
        kernel,
        out_shape=outs,
        in_specs=in_vmem(n_in),
        out_specs=[pl.BlockSpec(memory_space=pltpu.VMEM)] * len(outs),
        scratch_shapes=scratch,
        compiler_params=pltpu.CompilerParams(vmem_limit_bytes=VMEM),
        cost_estimate=pl.CostEstimate(flops=flops, bytes_accessed=6 << 20, transcendentals=0),
    )


def shape(dims, dtype):
    return jax.ShapeDtypeStruct(dims, dtype)


def swap(x, axis):
    return lax.ppermute(x, axis, [(0, 1), (1, 0)])


def turn(x, step):
    return lax.ppermute(x, "x", [(i, (i + step) % 4) for i in range(4)])


def along_z(x, step0, step1):
    pairs = [(2 * z, 2 * ((z + step0) % 8)) for z in range(8)]
    if step1 is not None:
        pairs += [(2 * z + 1, 2 * ((z + step1) % 8) + 1) for z in range(8)]
    return lax.ppermute(x, ("z", "c"), pairs)


def add(a, b):
    return a.astype(F32) + b.astype(F32)


def local(queries, key_states, value_vectors, grad_output, out_weight, doc_lengths):
    z, yl, c = lax.axis_index("z"), lax.axis_index("yl"), lax.axis_index("c")
    x, yh = lax.axis_index("x"), lax.axis_index("yh")
    first = c == 0
    pos0 = ((z * 2 + yl) * 2 + c) * 128

    kv = jnp.concatenate([key_states.reshape(128, HD), value_vectors.reshape(128, HD)], axis=1)
    other = swap(kv, "yl")
    half = jnp.where(yl == 0, jnp.concatenate([kv, other]), jnp.concatenate([other, kv]))
    other = swap(half, "c")
    plane = jnp.where(first, jnp.concatenate([half, other]), jnp.concatenate([other, half]))

    own, mate = out_weight, swap(out_weight, "c")
    weights = [own]
    w_own, w_mate, kv_step = own, mate, plane
    kv_got = []
    for step in range(3):
        w_own = along_z(w_own, 1, 7)
        w_mate = along_z(w_mate, 1, 7)
        weights += [w_own, w_mate]
        kv_step = along_z(kv_step, 1, (5, 7, None)[step])
        kv_got.append(kv_step)
    weights.append(along_z(w_own, 1, 7))

    rolled = lax.dynamic_slice(
        jnp.concatenate([grad_output, grad_output], axis=1), (0, z * 1024), (16, 8192)
    )

    def columns(to_yl, to_c):
        order = [(0, to_c)]
        for s in (1, 2, 3):
            far = s if to_c else 8 - s
            order += [(far, to_c), (far, 1 - to_c)]
        order.append((4, to_c))
        return jnp.concatenate(
            [rolled[:, s * 1024 + to_yl * 512 + par * 256 :][:, :256] for s, par in order], axis=1
        )

    sent = jnp.concatenate([columns(a, b) for a in (0, 1) for b in (0, 1)])
    got = lax.all_to_all(sent, ("yl", "c"), 0, 0, tiled=True)
    gh = jnp.concatenate([got, swap(got, "yh")])
    gu, gd = turn(gh, 1), turn(gh, 3)
    gu2, gd2 = turn(gu[:64], 1), turn(gd[64:], 3)

    me = jnp.stack([yl * 2 + c]).astype(jnp.int32)
    send, keep = call(
        project_kernel,
        13,
        [shape((2, 128, 1024), BF), shape((2, 128, 1024), F32)],
        [pltpu.VMEM((512, 2048), BF)],
        2 * 512 * 2048 * 1024,
    )(me, gh, gu, gd, gu2, gd2, *weights)
    both = keep + swap(send, "c").astype(F32)
    out_grad = (both[0] + swap(both[1].astype(BF), "yl").astype(F32)).astype(BF)

    ends = jnp.cumsum(doc_lengths)
    row_pos = pos0 + jnp.arange(128, dtype=jnp.int32)
    start = jnp.max(jnp.where(ends[None, :] <= row_pos[:, None], ends[None, :], 0), axis=1)
    count = z - start[0] // PLANE + 1
    starts = jnp.tile(start, 8).reshape(1, ROWS)
    scalars = jnp.stack([z, count, pos0, c, x, yh]).astype(jnp.int32)

    mine = jnp.stack(kv_got)
    theirs = swap(mine, "c")
    planes = jnp.concatenate(
        [
            plane[None],
            jnp.where(first, mine, theirs),
            jnp.where(first, theirs, mine)[1::-1],
        ]
    )
    q = queries.transpose(1, 0, 2).reshape(ROWS, HD)
    att, lse = call(
        forward_kernel,
        3,
        [shape((HD, ROWS), F32), shape((1, ROWS), F32)],
        [pltpu.VMEM((1, ROWS), F32)] * 2,
        4 * 1024 * 2560 * 128,
    )(scalars, q, planes, starts)

    dq, keep, send = call(
        backward_kernel,
        6,
        [shape((128, 1024), BF), shape((3, PLANE, 2 * HD), BF), shape((3, PLANE, 2 * HD), BF)],
        [
            pltpu.VMEM((ROWS, HD), BF),
            pltpu.VMEM((1, ROWS), F32),
            pltpu.VMEM((HD, ROWS), F32),
            pltpu.VMEM((PLANE, HD), F32),
            pltpu.VMEM((PLANE, HD), F32),
        ],
        10 * 1024 * 2560 * 128,
    )(scalars, q, out_grad, att, lse, planes, starts)

    terms = add(keep, swap(send, "c")).astype(BF)
    run = along_z(jnp.where(first, terms[2], terms[0]), 7, 1)
    run = along_z(add(run, terms[1]).astype(BF), 7, 3)
    run = add(run, jnp.where(first, terms[0], terms[2])).astype(BF)
    last = along_z(run, 7, None)
    run = jnp.where(first, last, run)
    total = add(
        jnp.where(first, run[:256], run[256:]),
        swap(jnp.where(first, run[256:], run[:256]), "c"),
    )
    there = swap(jnp.where(yl == 0, total[128:], total[:128]).astype(BF), "yl")
    kv_grad = (jnp.where(yl == 0, total[:128], total[128:]) + there.astype(F32)).astype(BF)
    return (
        dq.reshape(128, 8, HD),
        kv_grad[:, :HD].reshape(128, 1, HD),
        kv_grad[:, HD:].reshape(128, 1, HD),
    )


def solution(mesh):
    grid = Mesh(mesh.devices.reshape(8, 2, 2, 4, 2), ("z", "yl", "c", "x", "yh"))
    ctx, tp = ("z", "yl", "c"), ("x", "yh")
    return jax.shard_map(
        local,
        mesh=grid,
        in_specs=(
            P(ctx, tp, None),
            P(ctx, tp, None),
            P(ctx, tp, None),
            P(ctx + tp, None),
            P(ctx, tp),
            P(),
        ),
        out_specs=(P(ctx, tp, None), P(ctx, tp, None), P(ctx, tp, None)),
        check_vma=False,
    )
```

```python
import math

import jax
import jax.numpy as jnp
from jax import lax
from jax.experimental import pallas as pl
from jax.experimental.pallas import tpu as pltpu
from jax.sharding import Mesh, PartitionSpec as P

BF = jnp.bfloat16
F32 = jnp.float32
NEG = -1e30
HD = 128
SCALE = HD**-0.5
C2 = SCALE * math.log2(math.e)
PLANE = 512
PLANES = 6
ROWS = 1024
MIB = 1024 * 1024
P_MIB, F_MIB, B_MIB = 16, 20, 24
HINT = 8

NT = (((1,), (1,)), ((), ()))
NN = (((1,), (0,)), ((), ()))
TN = (((0,), (0,)), ((), ()))


def dot(a, b, dims):
    return lax.dot_general(a, b, dims, preferred_element_type=F32)


def key_positions(z, d):
    r = lax.broadcasted_iota(jnp.int32, (PLANE, 1), 0)
    part = r >> 7
    block = ((part & 1) << 1) | (part >> 1)
    return (z - d) * PLANE + block * 128 + (r & 127)


def where_am_i():
    z, c = lax.axis_index("z"), lax.axis_index("c")
    return z, c, ((z * 2 + lax.axis_index("yl")) * 2 + c) * 128


def documents(lengths, pos0):
    row_pos = pos0 + (lax.broadcasted_iota(jnp.int32, (1, ROWS), 1) & 127)
    start, low, high = jnp.zeros((1, ROWS), jnp.int32), 0, 0
    end = lengths[0]
    for i in range(8):
        start = jnp.where(end <= row_pos, end, start)
        low = jnp.where(end <= pos0, end, low)
        high = jnp.where(end <= pos0 + 127, end, high)
        if i < 7:
            end = end + lengths[i + 1]
    return row_pos, start, low, high


def project_kernel(gh, gu, gd, gu2, gd2, w0, w1, w2, w3, w4, total, rest, a_scr):
    me = lax.axis_index("yl") * 2 + lax.axis_index("c")
    x, yh = lax.axis_index("x"), lax.axis_index("yh")
    for rel in range(4):
        src = pl.multiple_of((me ^ rel) * 16, 16)
        for half in range(2):
            base = pl.multiple_of(src + half * 64, 16)
            for turn_by, ref, at in (
                (0, gh, base),
                (1, gd, base),
                (2, (gu2, gd2)[half], src),
                (3, gu, base),
            ):
                tp = ((x + turn_by) & 3) * 2 + (yh ^ half)
                row = pl.multiple_of(rel * 128 + tp * 16, 16)
                a_scr[pl.ds(row, 16), :] = ref[pl.ds(at, 16), 0:1280]
                rest[pl.ds(row, 16), :] = ref[pl.ds(at, 16), 1280:2048]
    out = None
    for k, w in enumerate((w0, w1, w2, w3, w4)):
        part = dot(a_scr[:, k * 256 : k * 256 + 256], w[...], NN)
        out = part if out is None else out + part
    total[...] = out


def forward_kernel(
    lengths, q, plane, r1, r2, r3, t1, t2, t3, att, lse, kv, m_scr, l_scr
):
    z, c, pos0 = where_am_i()
    row_pos, start, low, high = documents(lengths, pos0)

    def place(d, ref):
        for b in range(4):
            kv[d, b * 128 : b * 128 + 128, :] = ref[:, b * 256 : b * 256 + 256]

    def place_all(near, far):
        for d, ref in ((1, near[0]), (2, near[1]), (3, near[2]), (4, far[1]), (5, far[0])):
            place(d, ref)

    place(0, plane)

    @pl.when(c == 0)
    def _():
        place_all((r1, r2, r3), (t1, t2))

    @pl.when(c != 0)
    def _():
        place_all((t1, t2, t3), (r1, r2))

    m_scr[...] = jnp.full((1, ROWS), NEG, F32)
    l_scr[...] = jnp.zeros((1, ROWS), F32)
    att[...] = jnp.zeros((HD, ROWS), F32)

    def work(d, masked):
        k = kv[d, :, 0:HD]
        v_t = kv[d, :, HD : 2 * HD].astype(F32).T.astype(BF)
        s = dot(k, q[...], NT)
        if masked:
            s = jnp.where(allowed(z, d, row_pos, start), s, NEG)
        old = m_scr[...]
        new = jnp.maximum(old, jnp.max(s, axis=0, keepdims=True) * C2)
        shrink = jnp.exp2(old - new)
        p = jnp.exp2(s * C2 - new)
        l_scr[...] = l_scr[...] * shrink + jnp.sum(p, axis=0, keepdims=True)
        m_scr[...] = new
        att[...] = att[...] * shrink + dot(v_t, p.astype(BF), NN)

    each_plane(work, z, 0, z - low // PLANE + 1, high)
    lse[...] = m_scr[...] + jnp.log2(l_scr[...])
    att[...] = att[...] / l_scr[...]


def allowed(z, d, row_pos, start):
    keys = key_positions(z, d)
    return (keys >= start) & (keys <= row_pos)


def each_plane(work, z, begin, end, clear):
    def plane(d, carry):
        whole = (d > 0) & ((z - d) * PLANE >= clear)

        @pl.when(whole)
        def _():
            work(d, False)

        @pl.when(jnp.logical_not(whole))
        def _():
            work(d, True)

        return carry

    lax.fori_loop(begin, end, plane, 0)


def gradients(lengths, q, do, kv, lse, delta, dq_t, begin, end, store):
    z, c, pos0 = where_am_i()
    row_pos, start, low, high = documents(lengths, pos0)
    count = z - low // PLANE + 1

    def work(d, masked):
        k = kv[d, :, 0:HD]
        v = kv[d, :, HD : 2 * HD]
        k_t = k.astype(F32).T.astype(BF)
        s = dot(k, q[...], NT)
        dp = dot(v, do[...], NT)
        p = jnp.exp2(s * C2 - lse[...])
        if masked:
            p = jnp.where(allowed(z, d, row_pos, start), p, 0.0)
        dv = dot(p.astype(BF), do[...], NN)
        ds = (p * (dp - delta[...])).astype(BF)
        dk = dot(ds, q[...], NN) * SCALE
        dq_t[...] += dot(k_t, ds, NN)
        store(d, jnp.concatenate([dk, dv], axis=1).astype(BF))

    stop = jnp.clip(count, begin, end)
    each_plane(work, z, begin, stop, high)

    def blank(d, carry):
        store(d, jnp.zeros((PLANE, 2 * HD), BF))
        return carry

    lax.fori_loop(stop, end, blank, 0)


def far_kernel(
    lengths, q, o0, o1, o2, att, lse, kv, keep, send, fifth, do, delta, dq_t
):
    c = lax.axis_index("c")
    o = (o0[...] + o1[...].astype(F32) + o2[...].astype(F32)).astype(BF)
    for h in range(8):
        cols = slice(h * 128, h * 128 + 128)
        do[cols, :] = o[:, cols]
        delta[:, cols] = jnp.sum(o[:, cols].astype(F32).T * att[:, cols], axis=0, keepdims=True)
    dq_t[...] = jnp.zeros((HD, ROWS), F32)

    def store(d, value):
        mine = ((d == 3) & (c == 0)) | ((d == 4) & (c != 0))

        @pl.when(mine)
        def _():
            keep[...] = value

        @pl.when((d < 5) & jnp.logical_not(mine))
        def _():
            send[...] = value

        @pl.when(d == 5)
        def _():
            fifth[...] = value

    gradients(lengths, q, do, kv, lse, delta, dq_t, 3, 6, store)


def near_kernel(
    lengths, q, do, lse, delta, kv, dq_far, fifth, dq, keep2, keep1, send2, send1, dq_t
):
    c = lax.axis_index("c")
    dq_t[...] = dq_far[...]

    @pl.when(c == 0)
    def _():
        send2[...] = fifth[...]

    @pl.when(c != 0)
    def _():
        keep2[...] = fifth[...]

    def store(d, value):
        @pl.when((d == 2) & (c == 0))
        def _():
            keep2[...] = value

        @pl.when((d == 2) & (c != 0))
        def _():
            send2[...] = value

        mine = ((d == 1) & (c == 0)) | ((d == 0) & (c != 0))

        @pl.when(mine)
        def _():
            keep1[...] = value

        @pl.when((d < 2) & jnp.logical_not(mine))
        def _():
            send1[...] = value

    gradients(lengths, q, do, kv, lse, delta, dq_t, 0, 3, store)
    for h in range(8):
        cols = slice(h * 128, h * 128 + 128)
        dq[:, cols] = (dq_t[:, cols] * SCALE).T.astype(BF)


def call(kernel, args, outs, scratch, flops, vmem_mib, scalars=None):
    vmem = pl.BlockSpec(memory_space=pltpu.VMEM)
    first = [] if scalars is None else [pl.BlockSpec(memory_space=pltpu.SMEM)]
    return pl.pallas_call(
        kernel,
        out_shape=outs,
        in_specs=first + [vmem] * len(args),
        out_specs=[vmem] * len(outs),
        scratch_shapes=scratch,
        compiler_params=pltpu.CompilerParams(vmem_limit_bytes=vmem_mib * MIB),
        cost_estimate=pl.CostEstimate(flops=flops, bytes_accessed=6 << 20, transcendentals=0),
    )(*([] if scalars is None else [scalars]), *args)


def tie(*xs):
    return lax.optimization_barrier(xs)


def shape(dims, dtype):
    return jax.ShapeDtypeStruct(dims, dtype)


def swap(x, axis):
    return lax.ppermute(x, axis, [(0, 1), (1, 0)])


def turn(x, step):
    return lax.ppermute(x, "x", [(i, (i + step) % 4) for i in range(4)])


def along_z(x, step0, step1):
    pairs = [(2 * z, 2 * ((z + step0) % 8)) for z in range(8)]
    if step1 is not None:
        pairs += [(2 * z + 1, 2 * ((z + step1) % 8) + 1) for z in range(8)]
    return lax.ppermute(x, ("z", "c"), pairs)


def add(a, b):
    return a.astype(F32) + b.astype(F32)


def local(queries, key_states, value_vectors, grad_output, out_weight, doc_lengths):
    z, yl, c = lax.axis_index("z"), lax.axis_index("yl"), lax.axis_index("c")
    first = c == 0

    rolled = lax.dynamic_slice(
        jnp.concatenate([grad_output, grad_output], axis=1), (0, z * 1024), (16, 8192)
    )

    def columns(to_yl, to_c):
        order = [(0, to_c)]
        for s in (1, 2, 3):
            far = s if to_c else 8 - s
            order += [(far, to_c), (far, 1 - to_c)]
        order.append((4, to_c))
        return jnp.concatenate(
            [rolled[:, s * 1024 + to_yl * 512 + par * 256 :][:, :256] for s, par in order], axis=1
        )

    sent = jnp.stack([columns(a, b) for a in (0, 1) for b in (0, 1)])

    t = swap(jnp.where(first, sent[1::2], sent[0::2]).reshape(32, 2048), "c")
    own = jnp.where(first, sent[0::2], sent[1::2]).reshape(32, 2048)
    both = jnp.where(first, jnp.stack([own, t]), jnp.stack([t, own])).reshape(2, 2, 16, 2048)
    away = swap(jnp.where(yl == 0, both[:, 1], both[:, 0]), "yl")
    here = jnp.where(yl == 0, both[:, 0], both[:, 1])
    got = jnp.where(yl == 0, jnp.stack([here, away]), jnp.stack([away, here])).reshape(64, 2048)
    gh = jnp.concatenate([got, swap(got, "yh")])
    gu, gd = turn(gh, 1), turn(gh, 3)
    gu2, gd2 = turn(gu[:64], 1), turn(gd[64:], 3)

    p1 = along_z(out_weight, 1, 7)
    q0 = swap(out_weight, "c")
    kv = jnp.concatenate([key_states.reshape(128, HD), value_vectors.reshape(128, HD)], axis=1)
    other = swap(kv, "yl")
    half = jnp.where(
        yl == 0, jnp.concatenate([kv, other], axis=1), jnp.concatenate([other, kv], axis=1)
    )
    other = swap(half, "c")
    plane = jnp.where(
        first, jnp.concatenate([half, other], axis=1), jnp.concatenate([other, half], axis=1)
    )
    q1 = along_z(q0, 1, 7)
    r1 = along_z(plane, 1, 5)
    p2 = along_z(p1, 1, 7)
    q2 = along_z(q1, 1, 7)
    r2 = along_z(tie(r1, q1, p2)[0], 1, 7)
    p3 = along_z(p2, 1, 7)
    q3 = along_z(q2, 1, 7)
    r3 = along_z(r2, 1, None)
    p4 = along_z(p3, 1, 7)

    t1, t2, t3 = swap(r1, "c"), swap(r2, "c"), swap(r3, "c")

    total, rest = call(
        project_kernel,
        [gh, gu, gd, gu2, gd2, out_weight, p1, q1, p2, q2],
        [shape((512, 1024), F32), shape((512, 768), BF)],
        [pltpu.VMEM((512, 1280), BF)],
        HINT * 2 * 512 * 1280 * 1024,
        P_MIB,
    )
    for k, w in enumerate((p3, q3, p4)):
        total = total + dot(rest[:, k * 256 : k * 256 + 256], w, NN)
    total = total.reshape(2, 2, 128, 1024)
    keep0, keep1 = total[0, 0], total[1, 0]
    send, t3 = tie(total[1, 1].astype(BF), t3)
    from_both = swap(send, "c")
    from_core = swap(total[0, 1].astype(BF), "c")
    from_y = swap(add(keep1, from_both).astype(BF), "yl")

    q = queries.transpose(1, 0, 2).reshape(ROWS, HD)
    q, from_both = tie(q, from_both)
    att, lse, planes = call(
        forward_kernel,
        [q, plane, r1, r2, r3, t1, t2, t3],
        [
            shape((HD, ROWS), F32),
            shape((1, ROWS), F32),
            shape((PLANES, PLANE, 2 * HD), BF),
        ],
        [pltpu.VMEM((1, ROWS), F32)] * 2,
        1,
        F_MIB,
        doc_lengths,
    )

    block = shape((PLANE, 2 * HD), BF)
    keep, send, fifth, do, delta, dq_far = call(
        far_kernel,
        [q, keep0, from_core, from_y, att, lse, planes],
        [block, block, block, shape((ROWS, HD), BF), shape((1, ROWS), F32), shape((HD, ROWS), F32)],
        [],
        5 * 1024 * 2560 * 128,
        B_MIB,
        doc_lengths,
    )

    got = swap(send, "c")
    run = along_z(add(keep, got).astype(BF), 7, 1)
    q, got = tie(q, got)
    dq, keep2, keep1, send2, send1 = call(
        near_kernel,
        [q, do, lse, delta, planes, dq_far, fifth],
        [shape((128, 1024), BF), block, block, block, block],
        [pltpu.VMEM((HD, ROWS), F32)],
        5 * 1024 * 2560 * 128,
        B_MIB,
        doc_lengths,
    )
    middle = add(keep2, swap(send2, "c"))
    final = add(keep1, swap(send1, "c"))
    run = along_z((run.astype(F32) + middle).astype(BF), 7, 2)
    run = jnp.where(first, run.astype(F32) + final, run.astype(F32)).astype(BF)
    run = along_z(run, 7, 1)
    run = jnp.where(first, run.astype(F32), run.astype(F32) + final)
    total = jnp.where(first, run[:256], run[256:]) + swap(
        jnp.where(first, run[256:], run[:256]).astype(BF), "c"
    ).astype(F32)
    there = swap(jnp.where(yl == 0, total[128:], total[:128]).astype(BF), "yl")
    kv_grad = (jnp.where(yl == 0, total[:128], total[128:]) + there.astype(F32)).astype(BF)
    return (
        dq.reshape(128, 8, HD),
        kv_grad[:, :HD].reshape(128, 1, HD),
        kv_grad[:, HD:].reshape(128, 1, HD),
    )


def solution(mesh):
    grid = Mesh(mesh.devices.reshape(8, 2, 2, 4, 2), ("z", "yl", "c", "x", "yh"))
    ctx, tp = ("z", "yl", "c"), ("x", "yh")
    return jax.shard_map(
        local,
        mesh=grid,
        in_specs=(
            P(ctx, tp, None),
            P(ctx, tp, None),
            P(ctx, tp, None),
            P(ctx + tp, None),
            P(ctx, tp),
            P(),
        ),
        out_specs=(P(ctx, tp, None), P(ctx, tp, None), P(ctx, tp, None)),
        check_vma=False,
    )
```

```python
import math

import jax
import jax.numpy as jnp
from jax import lax
from jax.experimental import pallas as pl
from jax.experimental.pallas import tpu as pltpu
from jax.sharding import Mesh, PartitionSpec as P

BF = jnp.bfloat16
F32 = jnp.float32
NEG = -1e30
HD = 128
SCALE = HD**-0.5
C2 = SCALE * math.log2(math.e)
PLANE = 512
PLANES = 6
ROWS = 1024
MIB = 1024 * 1024
P_MIB, F_MIB, B_MIB = 16, 20, 24
HINT = 0

NT = (((1,), (1,)), ((), ()))
NN = (((1,), (0,)), ((), ()))
TN = (((0,), (0,)), ((), ()))


def dot(a, b, dims):
    return lax.dot_general(a, b, dims, preferred_element_type=F32)


def key_positions(z, d):
    r = lax.broadcasted_iota(jnp.int32, (PLANE, 1), 0)
    part = r >> 7
    block = ((part & 1) << 1) | (part >> 1)
    return (z - d) * PLANE + block * 128 + (r & 127)


def where_am_i():
    z, c = lax.axis_index("z"), lax.axis_index("c")
    return z, c, ((z * 2 + lax.axis_index("yl")) * 2 + c) * 128


def documents(lengths, pos0):
    row_pos = pos0 + (lax.broadcasted_iota(jnp.int32, (1, ROWS), 1) & 127)
    start, low, high = jnp.zeros((1, ROWS), jnp.int32), 0, 0
    end = lengths[0]
    for i in range(8):
        start = jnp.where(end <= row_pos, end, start)
        low = jnp.where(end <= pos0, end, low)
        high = jnp.where(end <= pos0 + 127, end, high)
        if i < 7:
            end = end + lengths[i + 1]
    return row_pos, start, low, high


def project_kernel(gh, gu, gd, gu2, gd2, w0, w1, w2, w3, w4, total, rest, a_scr):
    me = lax.axis_index("yl") * 2 + lax.axis_index("c")
    x, yh = lax.axis_index("x"), lax.axis_index("yh")
    for rel in range(4):
        src = pl.multiple_of((me ^ rel) * 16, 16)
        for half in range(2):
            base = pl.multiple_of(src + half * 64, 16)
            for turn_by, ref, at in (
                (0, gh, base),
                (1, gd, base),
                (2, (gu2, gd2)[half], src),
                (3, gu, base),
            ):
                tp = ((x + turn_by) & 3) * 2 + (yh ^ half)
                row = pl.multiple_of(rel * 128 + tp * 16, 16)
                a_scr[pl.ds(row, 16), :] = ref[pl.ds(at, 16), 0:1280]
                rest[pl.ds(row, 16), :] = ref[pl.ds(at, 16), 1280:2048]
    out = None
    for k, w in enumerate((w0, w1, w2, w3, w4)):
        part = dot(a_scr[:, k * 256 : k * 256 + 256], w[...], NN)
        out = part if out is None else out + part
    total[...] = out


def forward_kernel(
    lengths, q, plane, r1, r2, r3, t1, t2, t3, att, lse, kv, m_scr, l_scr
):
    z, c, pos0 = where_am_i()
    row_pos, start, low, high = documents(lengths, pos0)

    def place(d, ref):
        for b in range(4):
            kv[d, b * 128 : b * 128 + 128, :] = ref[:, b * 256 : b * 256 + 256]

    def place_all(near, far):
        for d, ref in ((1, near[0]), (2, near[1]), (3, near[2]), (4, far[1]), (5, far[0])):
            place(d, ref)

    place(0, plane)

    @pl.when(c == 0)
    def _():
        place_all((r1, r2, r3), (t1, t2))

    @pl.when(c != 0)
    def _():
        place_all((t1, t2, t3), (r1, r2))

    m_scr[...] = jnp.full((1, ROWS), NEG, F32)
    l_scr[...] = jnp.zeros((1, ROWS), F32)
    att[...] = jnp.zeros((HD, ROWS), F32)

    def work(d, masked):
        k = kv[d, :, 0:HD]
        v_t = kv[d, :, HD : 2 * HD].astype(F32).T.astype(BF)
        s = dot(k, q[...], NT)
        if masked:
            s = jnp.where(allowed(z, d, row_pos, start), s, NEG)
        old = m_scr[...]
        new = jnp.maximum(old, jnp.max(s, axis=0, keepdims=True) * C2)
        shrink = jnp.exp2(old - new)
        p = jnp.exp2(s * C2 - new)
        l_scr[...] = l_scr[...] * shrink + jnp.sum(p, axis=0, keepdims=True)
        m_scr[...] = new
        att[...] = att[...] * shrink + dot(v_t, p.astype(BF), NN)

    each_plane(work, z, 0, z - low // PLANE + 1, high)
    lse[...] = m_scr[...] + jnp.log2(l_scr[...])
    att[...] = att[...] / l_scr[...]


def allowed(z, d, row_pos, start):
    keys = key_positions(z, d)
    return (keys >= start) & (keys <= row_pos)


def each_plane(work, z, begin, end, clear):
    def plane(d, carry):
        whole = (d > 0) & ((z - d) * PLANE >= clear)

        @pl.when(whole)
        def _():
            work(d, False)

        @pl.when(jnp.logical_not(whole))
        def _():
            work(d, True)

        return carry

    lax.fori_loop(begin, end, plane, 0)


def gradients(lengths, q, do, kv, lse, delta, dq_t, begin, end, store):
    z, c, pos0 = where_am_i()
    row_pos, start, low, high = documents(lengths, pos0)
    count = z - low // PLANE + 1

    def work(d, masked):
        k = kv[d, :, 0:HD]
        v = kv[d, :, HD : 2 * HD]
        k_t = k.astype(F32).T.astype(BF)
        s = dot(k, q[...], NT)
        dp = dot(v, do[...], NT)
        p = jnp.exp2(s * C2 - lse[...])
        if masked:
            p = jnp.where(allowed(z, d, row_pos, start), p, 0.0)
        dv = dot(p.astype(BF), do[...], NN)
        ds = (p * (dp - delta[...])).astype(BF)
        dk = dot(ds, q[...], NN) * SCALE
        dq_t[...] += dot(k_t, ds, NN)
        store(d, jnp.concatenate([dk, dv], axis=1).astype(BF))

    stop = jnp.clip(count, begin, end)
    each_plane(work, z, begin, stop, high)

    def blank(d, carry):
        store(d, jnp.zeros((PLANE, 2 * HD), BF))
        return carry

    lax.fori_loop(stop, end, blank, 0)


def far_kernel(
    lengths, q, o0, o1, o2, att, lse, kv, keep, send, fifth, do, delta, dq_t
):
    c = lax.axis_index("c")
    o = (o0[...] + o1[...].astype(F32) + o2[...].astype(F32)).astype(BF)
    for h in range(8):
        cols = slice(h * 128, h * 128 + 128)
        do[cols, :] = o[:, cols]
        delta[:, cols] = jnp.sum(o[:, cols].astype(F32).T * att[:, cols], axis=0, keepdims=True)
    dq_t[...] = jnp.zeros((HD, ROWS), F32)

    def store(d, value):
        mine = ((d == 3) & (c == 0)) | ((d == 4) & (c != 0))

        @pl.when(mine)
        def _():
            keep[...] = value

        @pl.when((d < 5) & jnp.logical_not(mine))
        def _():
            send[...] = value

        @pl.when(d == 5)
        def _():
            fifth[...] = value

    gradients(lengths, q, do, kv, lse, delta, dq_t, 3, 6, store)


def near_kernel(
    lengths, q, do, lse, delta, kv, dq_far, fifth, dq, keep2, keep1, send2, send1, dq_t
):
    c = lax.axis_index("c")
    dq_t[...] = dq_far[...]

    @pl.when(c == 0)
    def _():
        send2[...] = fifth[...]

    @pl.when(c != 0)
    def _():
        keep2[...] = fifth[...]

    def store(d, value):
        @pl.when((d == 2) & (c == 0))
        def _():
            keep2[...] = value

        @pl.when((d == 2) & (c != 0))
        def _():
            send2[...] = value

        mine = ((d == 1) & (c == 0)) | ((d == 0) & (c != 0))

        @pl.when(mine)
        def _():
            keep1[...] = value

        @pl.when((d < 2) & jnp.logical_not(mine))
        def _():
            send1[...] = value

    gradients(lengths, q, do, kv, lse, delta, dq_t, 0, 3, store)
    for h in range(8):
        cols = slice(h * 128, h * 128 + 128)
        dq[:, cols] = (dq_t[:, cols] * SCALE).T.astype(BF)


def call(kernel, args, outs, scratch, flops, vmem_mib, scalars=None):
    vmem = pl.BlockSpec(memory_space=pltpu.VMEM)
    first = [] if scalars is None else [pl.BlockSpec(memory_space=pltpu.SMEM)]
    return pl.pallas_call(
        kernel,
        out_shape=outs,
        in_specs=first + [vmem] * len(args),
        out_specs=[vmem] * len(outs),
        scratch_shapes=scratch,
        compiler_params=pltpu.CompilerParams(vmem_limit_bytes=vmem_mib * MIB),
        cost_estimate=pl.CostEstimate(flops=flops, bytes_accessed=6 << 20, transcendentals=0),
    )(*([] if scalars is None else [scalars]), *args)


def tie(*xs):
    return lax.optimization_barrier(xs)


def shape(dims, dtype):
    return jax.ShapeDtypeStruct(dims, dtype)


def swap(x, axis):
    return lax.ppermute(x, axis, [(0, 1), (1, 0)])


def turn(x, step):
    return lax.ppermute(x, "x", [(i, (i + step) % 4) for i in range(4)])


def along_z(x, step0, step1):
    pairs = [(2 * z, 2 * ((z + step0) % 8)) for z in range(8)]
    if step1 is not None:
        pairs += [(2 * z + 1, 2 * ((z + step1) % 8) + 1) for z in range(8)]
    return lax.ppermute(x, ("z", "c"), pairs)


def add(a, b):
    return a.astype(F32) + b.astype(F32)


def local(queries, key_states, value_vectors, grad_output, out_weight, doc_lengths):
    z, yl, c = lax.axis_index("z"), lax.axis_index("yl"), lax.axis_index("c")
    first = c == 0

    rolled = lax.dynamic_slice(
        jnp.concatenate([grad_output, grad_output], axis=1), (0, z * 1024), (16, 8192)
    )

    def columns(to_yl, to_c):
        order = [(0, to_c)]
        for s in (1, 2, 3):
            far = s if to_c else 8 - s
            order += [(far, to_c), (far, 1 - to_c)]
        order.append((4, to_c))
        return jnp.concatenate(
            [rolled[:, s * 1024 + to_yl * 512 + par * 256 :][:, :256] for s, par in order], axis=1
        )

    sent = jnp.stack([columns(a, b) for a in (0, 1) for b in (0, 1)])

    t = swap(jnp.where(first, sent[1::2], sent[0::2]).reshape(32, 2048), "c")
    own = jnp.where(first, sent[0::2], sent[1::2]).reshape(32, 2048)
    both = jnp.where(first, jnp.stack([own, t]), jnp.stack([t, own])).reshape(2, 2, 16, 2048)
    q0 = swap(out_weight, "c")
    both, q0 = tie(both, q0)
    away = swap(jnp.where(yl == 0, both[:, 1], both[:, 0]), "yl")
    here = jnp.where(yl == 0, both[:, 0], both[:, 1])
    got = jnp.where(yl == 0, jnp.stack([here, away]), jnp.stack([away, here])).reshape(64, 2048)
    gh = jnp.concatenate([got, swap(got, "yh")])
    gu, gd = turn(gh, 1), turn(gh, 3)
    gu2, gd2 = turn(gu[:64], 1), turn(gd[64:], 3)

    p1 = along_z(out_weight, 1, 7)
    kv = jnp.concatenate([key_states.reshape(128, HD), value_vectors.reshape(128, HD)], axis=1)
    other = swap(kv, "yl")
    half = jnp.where(
        yl == 0, jnp.concatenate([kv, other], axis=1), jnp.concatenate([other, kv], axis=1)
    )
    other = swap(half, "c")
    plane = jnp.where(
        first, jnp.concatenate([half, other], axis=1), jnp.concatenate([other, half], axis=1)
    )
    q1 = along_z(q0, 1, 7)
    r1 = along_z(plane, 1, 5)
    p2 = along_z(p1, 1, 7)
    q2 = along_z(q1, 1, 7)
    r2 = along_z(tie(r1, q1, p2)[0], 1, 7)
    p3 = along_z(p2, 1, 7)
    q3 = along_z(q2, 1, 7)
    r3 = along_z(r2, 1, None)
    p4 = along_z(p3, 1, 7)

    t1, t2, t3 = swap(r1, "c"), swap(r2, "c"), swap(r3, "c")

    total, rest = call(
        project_kernel,
        [gh, gu, gd, gu2, gd2, out_weight, p1, q1, p2, q2],
        [shape((512, 1024), F32), shape((512, 768), BF)],
        [pltpu.VMEM((512, 1280), BF)],
        HINT * 2 * 512 * 1280 * 1024,
        P_MIB,
    )
    for k, w in enumerate((p3, q3, p4)):
        total = total + dot(rest[:, k * 256 : k * 256 + 256], w, NN)
    total = total.reshape(2, 2, 128, 1024)
    keep0, keep1 = total[0, 0], total[1, 0]
    send, t3 = tie(total[1, 1].astype(BF), t3)
    from_both = swap(send, "c")
    from_core = swap(total[0, 1].astype(BF), "c")
    from_y = swap(add(keep1, from_both).astype(BF), "yl")

    q = queries.transpose(1, 0, 2).reshape(ROWS, HD)
    q, from_both = tie(q, from_both)
    att, lse, planes = call(
        forward_kernel,
        [q, plane, r1, r2, r3, t1, t2, t3],
        [
            shape((HD, ROWS), F32),
            shape((1, ROWS), F32),
            shape((PLANES, PLANE, 2 * HD), BF),
        ],
        [pltpu.VMEM((1, ROWS), F32)] * 2,
        1,
        F_MIB,
        doc_lengths,
    )

    block = shape((PLANE, 2 * HD), BF)
    keep, send, fifth, do, delta, dq_far = call(
        far_kernel,
        [q, keep0, from_core, from_y, att, lse, planes],
        [block, block, block, shape((ROWS, HD), BF), shape((1, ROWS), F32), shape((HD, ROWS), F32)],
        [],
        5 * 1024 * 2560 * 128,
        B_MIB,
        doc_lengths,
    )

    got = swap(send, "c")
    run = along_z(add(keep, got).astype(BF), 7, 1)
    q, got = tie(q, got)
    dq, keep2, keep1, send2, send1 = call(
        near_kernel,
        [q, do, lse, delta, planes, dq_far, fifth],
        [shape((128, 1024), BF), block, block, block, block],
        [pltpu.VMEM((HD, ROWS), F32)],
        5 * 1024 * 2560 * 128,
        B_MIB,
        doc_lengths,
    )
    middle = add(keep2, swap(send2, "c"))
    final = add(keep1, swap(send1, "c"))
    run = along_z((run.astype(F32) + middle).astype(BF), 7, 2)
    run = jnp.where(first, run.astype(F32) + final, run.astype(F32)).astype(BF)
    run = along_z(run, 7, 1)
    run = jnp.where(first, run.astype(F32), run.astype(F32) + final)
    total = jnp.where(first, run[:256], run[256:]) + swap(
        jnp.where(first, run[256:], run[:256]).astype(BF), "c"
    ).astype(F32)
    there = swap(jnp.where(yl == 0, total[128:], total[:128]).astype(BF), "yl")
    kv_grad = (jnp.where(yl == 0, total[:128], total[128:]) + there.astype(F32)).astype(BF)
    return (
        dq.reshape(128, 8, HD),
        kv_grad[:, :HD].reshape(128, 1, HD),
        kv_grad[:, HD:].reshape(128, 1, HD),
    )


def solution(mesh):
    grid = Mesh(mesh.devices.reshape(8, 2, 2, 4, 2), ("z", "yl", "c", "x", "yh"))
    ctx, tp = ("z", "yl", "c"), ("x", "yh")
    return jax.shard_map(
        local,
        mesh=grid,
        in_specs=(
            P(ctx, tp, None),
            P(ctx, tp, None),
            P(ctx, tp, None),
            P(ctx + tp, None),
            P(ctx, tp),
            P(),
        ),
        out_specs=(P(ctx, tp, None), P(ctx, tp, None), P(ctx, tp, None)),
        check_vma=False,
    )
```

```python
import math

import jax
import jax.numpy as jnp
from jax import lax
from jax.experimental import pallas as pl
from jax.experimental.pallas import tpu as pltpu
from jax.sharding import Mesh, PartitionSpec as P

BF = jnp.bfloat16
F32 = jnp.float32
NEG = -1e30
HD = 128
SCALE = HD**-0.5
C2 = SCALE * math.log2(math.e)
PLANE = 512
PLANES = 6
ROWS = 1024
MIB = 1024 * 1024
P_MIB, F_MIB, B_MIB = 16, 20, 24
HINT = 0

NT = (((1,), (1,)), ((), ()))
NN = (((1,), (0,)), ((), ()))
TN = (((0,), (0,)), ((), ()))


def dot(a, b, dims):
    return lax.dot_general(a, b, dims, preferred_element_type=F32)


def key_positions(z, d):
    r = lax.broadcasted_iota(jnp.int32, (PLANE, 1), 0)
    part = r >> 7
    block = ((part & 1) << 1) | (part >> 1)
    return (z - d) * PLANE + block * 128 + (r & 127)


def where_am_i():
    z, c = lax.axis_index("z"), lax.axis_index("c")
    return z, c, ((z * 2 + lax.axis_index("yl")) * 2 + c) * 128


def documents(lengths, pos0):
    row_pos = pos0 + (lax.broadcasted_iota(jnp.int32, (1, ROWS), 1) & 127)
    start, low, high = jnp.zeros((1, ROWS), jnp.int32), 0, 0
    end = lengths[0]
    for i in range(8):
        start = jnp.where(end <= row_pos, end, start)
        low = jnp.where(end <= pos0, end, low)
        high = jnp.where(end <= pos0 + 127, end, high)
        if i < 7:
            end = end + lengths[i + 1]
    return row_pos, start, low, high


def project_kernel(gh, gu, gd, gu2, gd2, w0, w1, w2, w3, w4, total, rest, a_scr):
    me = lax.axis_index("yl") * 2 + lax.axis_index("c")
    x, yh = lax.axis_index("x"), lax.axis_index("yh")
    for rel in range(4):
        src = pl.multiple_of((me ^ rel) * 16, 16)
        for half in range(2):
            base = pl.multiple_of(src + half * 64, 16)
            for turn_by, ref, at in (
                (0, gh, base),
                (1, gd, base),
                (2, (gu2, gd2)[half], src),
                (3, gu, base),
            ):
                tp = ((x + turn_by) & 3) * 2 + (yh ^ half)
                row = pl.multiple_of(rel * 128 + tp * 16, 16)
                a_scr[pl.ds(row, 16), :] = ref[pl.ds(at, 16), 0:1280]
                rest[pl.ds(row, 16), :] = ref[pl.ds(at, 16), 1280:2048]
    out = None
    for k, w in enumerate((w0, w1, w2, w3, w4)):
        part = dot(a_scr[:, k * 256 : k * 256 + 256], w[...], NN)
        out = part if out is None else out + part
    total[...] = out


def forward_planes(lengths, q, kv, probs, tops, att, m_row, l_row):
    z, c, pos0 = where_am_i()
    row_pos, start, low, high = documents(lengths, pos0)

    def work(d, masked):
        k = kv[d, :, 0:HD]
        v_t = kv[d, :, HD : 2 * HD].astype(F32).T.astype(BF)
        s = dot(k, q[...], NT)
        if masked:
            s = jnp.where(allowed(z, d, row_pos, start), s, NEG)
        old = m_row[...]
        new = jnp.maximum(old, jnp.max(s, axis=0, keepdims=True) * C2)
        shrink = jnp.exp2(old - new)
        p = jnp.exp2(s * C2 - new)
        l_row[...] = l_row[...] * shrink + jnp.sum(p, axis=0, keepdims=True)
        m_row[...] = new
        tops[d] = new
        p = p.astype(BF)
        probs[d] = p
        att[...] = att[...] * shrink + dot(v_t, p, NN)

    each_plane(work, z, 0, z - low // PLANE + 1, high)


def place(kv, i, ref):
    for b in range(4):
        kv[i, b * 128 : b * 128 + 128, :] = ref[:, b * 256 : b * 256 + 256]


def forward_kernel(
    lengths, q, plane, r1, r2, r3, t1, t2, t3, att, kv, probs, factors, m_row, l_row
):
    place(kv, 0, plane)

    @pl.when(lax.axis_index("c") == 0)
    def _():
        for i, ref in enumerate((r1, r2, r3, t2, t1)):
            place(kv, i + 1, ref)

    @pl.when(lax.axis_index("c") != 0)
    def _():
        for i, ref in enumerate((t1, t2, t3, r2, r1)):
            place(kv, i + 1, ref)

    m_row[...] = jnp.full((1, ROWS), NEG, F32)
    l_row[...] = jnp.zeros((1, ROWS), F32)
    att[...] = jnp.zeros((HD, ROWS), F32)
    factors[...] = jnp.zeros((PLANES, 1, ROWS), F32)
    forward_planes(lengths, q, kv, probs, factors, att, m_row, l_row)
    lse = m_row[...] + jnp.log2(l_row[...])
    for i in range(PLANES):
        factors[i] = jnp.exp2(jnp.minimum(factors[i] - lse, 0.0))
    att[...] = att[...] / l_row[...]


def allowed(z, d, row_pos, start):
    keys = key_positions(z, d)
    return (keys >= start) & (keys <= row_pos)


def each_plane(work, z, begin, end, clear):
    def plane(d, carry):
        whole = (d > 0) & ((z - d) * PLANE >= clear)

        @pl.when(whole)
        def _():
            work(d, False)

        @pl.when(jnp.logical_not(whole))
        def _():
            work(d, True)

        return carry

    lax.fori_loop(begin, end, plane, 0)


def gradients(lengths, q, do, kv, probs, factors, delta, dq_t, begin, store):
    z, c, pos0 = where_am_i()
    row_pos, start, low, high = documents(lengths, pos0)

    def plane(d, carry):
        k = kv[d, :, 0:HD]
        v = kv[d, :, HD : 2 * HD]
        k_t = k.astype(F32).T.astype(BF)
        p = probs[d].astype(F32) * factors[d]
        dv = dot(p.astype(BF), do[...], NN)
        dp = dot(v, do[...], NT)
        ds = (p * (dp - delta[...])).astype(BF)
        dk = dot(ds, q[...], NN) * SCALE
        dq_t[...] += dot(k_t, ds, NN)
        store(d, jnp.concatenate([dk, dv], axis=1).astype(BF))
        return carry

    stop = jnp.clip(z - low // PLANE + 1, begin, begin + 3)
    lax.fori_loop(begin, stop, plane, 0)

    def blank(d, carry):
        store(d, jnp.zeros((PLANE, 2 * HD), BF))
        return carry

    lax.fori_loop(stop, begin + 3, blank, 0)


def far_kernel(
    lengths, q, o0, o1, o2, att, kv, probs, factors, keep, send, fifth, do, delta, dq_t
):
    c = lax.axis_index("c")
    o = (o0[...] + o1[...].astype(F32) + o2[...].astype(F32)).astype(BF)
    for h in range(8):
        cols = slice(h * 128, h * 128 + 128)
        do[cols, :] = o[:, cols]
        delta[:, cols] = jnp.sum(o[:, cols].astype(F32).T * att[:, cols], axis=0, keepdims=True)
    dq_t[...] = jnp.zeros((HD, ROWS), F32)

    def store(d, value):
        mine = ((d == 3) & (c == 0)) | ((d == 4) & (c != 0))

        @pl.when(mine)
        def _():
            keep[...] = value

        @pl.when((d < 5) & jnp.logical_not(mine))
        def _():
            send[...] = value

        @pl.when(d == 5)
        def _():
            fifth[...] = value

    gradients(lengths, q, do, kv, probs, factors, delta, dq_t, 3, store)


def near_kernel(
    lengths, q, do, delta, kv, probs, factors, dq_far, fifth, dq, keep2, keep1, send2, send1, dq_t
):
    c = lax.axis_index("c")
    dq_t[...] = dq_far[...]

    @pl.when(c == 0)
    def _():
        send2[...] = fifth[...]

    @pl.when(c != 0)
    def _():
        keep2[...] = fifth[...]

    def store(d, value):
        @pl.when((d == 2) & (c == 0))
        def _():
            keep2[...] = value

        @pl.when((d == 2) & (c != 0))
        def _():
            send2[...] = value

        mine = ((d == 1) & (c == 0)) | ((d == 0) & (c != 0))

        @pl.when(mine)
        def _():
            keep1[...] = value

        @pl.when((d < 2) & jnp.logical_not(mine))
        def _():
            send1[...] = value

    gradients(lengths, q, do, kv, probs, factors, delta, dq_t, 0, store)
    for h in range(8):
        cols = slice(h * 128, h * 128 + 128)
        dq[:, cols] = (dq_t[:, cols] * SCALE).T.astype(BF)


def call(kernel, args, outs, scratch, flops, vmem_mib, scalars=None):
    vmem = pl.BlockSpec(memory_space=pltpu.VMEM)
    first = [] if scalars is None else [pl.BlockSpec(memory_space=pltpu.SMEM)]
    return pl.pallas_call(
        kernel,
        out_shape=outs,
        in_specs=first + [vmem] * len(args),
        out_specs=[vmem] * len(outs),
        scratch_shapes=scratch,
        compiler_params=pltpu.CompilerParams(vmem_limit_bytes=vmem_mib * MIB),
        cost_estimate=pl.CostEstimate(flops=flops, bytes_accessed=6 << 20, transcendentals=0),
    )(*([] if scalars is None else [scalars]), *args)


def tie(*xs):
    return lax.optimization_barrier(xs)


def shape(dims, dtype):
    return jax.ShapeDtypeStruct(dims, dtype)


def swap(x, axis):
    return lax.ppermute(x, axis, [(0, 1), (1, 0)])


def turn(x, step):
    return lax.ppermute(x, "x", [(i, (i + step) % 4) for i in range(4)])


def along_z(x, step0, step1):
    pairs = [(2 * z, 2 * ((z + step0) % 8)) for z in range(8)]
    if step1 is not None:
        pairs += [(2 * z + 1, 2 * ((z + step1) % 8) + 1) for z in range(8)]
    return lax.ppermute(x, ("z", "c"), pairs)


def add(a, b):
    return a.astype(F32) + b.astype(F32)


def local(queries, key_states, value_vectors, grad_output, out_weight, doc_lengths):
    z, yl, c = lax.axis_index("z"), lax.axis_index("yl"), lax.axis_index("c")
    first = c == 0

    rolled = lax.dynamic_slice(
        jnp.concatenate([grad_output, grad_output], axis=1), (0, z * 1024), (16, 8192)
    )

    def columns(to_yl, to_c):
        order = [(0, to_c)]
        for s in (1, 2, 3):
            far = s if to_c else 8 - s
            order += [(far, to_c), (far, 1 - to_c)]
        order.append((4, to_c))
        return jnp.concatenate(
            [rolled[:, s * 1024 + to_yl * 512 + par * 256 :][:, :256] for s, par in order], axis=1
        )

    sent = jnp.stack([columns(a, b) for a in (0, 1) for b in (0, 1)])

    t = swap(jnp.where(first, sent[1::2], sent[0::2]).reshape(32, 2048), "c")
    own = jnp.where(first, sent[0::2], sent[1::2]).reshape(32, 2048)
    both = jnp.where(first, jnp.stack([own, t]), jnp.stack([t, own])).reshape(2, 2, 16, 2048)
    q0 = swap(out_weight, "c")
    both, q0 = tie(both, q0)
    away = swap(jnp.where(yl == 0, both[:, 1], both[:, 0]), "yl")
    here = jnp.where(yl == 0, both[:, 0], both[:, 1])
    got = jnp.where(yl == 0, jnp.stack([here, away]), jnp.stack([away, here])).reshape(64, 2048)
    gh = jnp.concatenate([got, swap(got, "yh")])
    gu, gd = turn(gh, 1), turn(gh, 3)
    gu2, gd2 = turn(gu[:64], 1), turn(gd[64:], 3)

    p1 = along_z(out_weight, 1, 7)
    kv = jnp.concatenate([key_states.reshape(128, HD), value_vectors.reshape(128, HD)], axis=1)
    other = swap(kv, "yl")
    half = jnp.where(
        yl == 0, jnp.concatenate([kv, other], axis=1), jnp.concatenate([other, kv], axis=1)
    )
    other = swap(half, "c")
    plane = jnp.where(
        first, jnp.concatenate([half, other], axis=1), jnp.concatenate([other, half], axis=1)
    )
    q1 = along_z(q0, 1, 7)
    r1 = along_z(plane, 1, 5)
    p2 = along_z(p1, 1, 7)
    q2 = along_z(q1, 1, 7)
    r2 = along_z(tie(r1, q1, p2)[0], 1, 7)
    p3 = along_z(p2, 1, 7)
    q3 = along_z(q2, 1, 7)
    r3 = along_z(r2, 1, None)
    p4 = along_z(p3, 1, 7)

    t1, t2, t3 = swap(r1, "c"), swap(r2, "c"), swap(r3, "c")

    total, rest = call(
        project_kernel,
        [gh, gu, gd, gu2, gd2, out_weight, p1, q1, p2, q2],
        [shape((512, 1024), F32), shape((512, 768), BF)],
        [pltpu.VMEM((512, 1280), BF)],
        HINT * 2 * 512 * 1280 * 1024,
        P_MIB,
    )
    for k, w in enumerate((p3, q3, p4)):
        total = total + dot(rest[:, k * 256 : k * 256 + 256], w, NN)
    total = total.reshape(2, 2, 128, 1024)
    keep0, keep1 = total[0, 0], total[1, 0]
    send, t3 = tie(total[1, 1].astype(BF), t3)
    from_both = swap(send, "c")
    from_core = swap(total[0, 1].astype(BF), "c")
    from_y = swap(add(keep1, from_both).astype(BF), "yl")

    q = queries.transpose(1, 0, 2).reshape(ROWS, HD)
    q, from_both = tie(q, from_both)
    row_shape, dq_shape = shape((1, ROWS), F32), shape((HD, ROWS), F32)
    att, kv, probs, factors = call(
        forward_kernel,
        [q, plane, r1, r2, r3, t1, t2, t3],
        [
            dq_shape,
            shape((PLANES, PLANE, 2 * HD), BF),
            shape((PLANES, PLANE, ROWS), BF),
            shape((PLANES, 1, ROWS), F32),
        ],
        [pltpu.VMEM((1, ROWS), F32)] * 2,
        1,
        F_MIB,
        doc_lengths,
    )

    block = shape((PLANE, 2 * HD), BF)
    keep, send, fifth, do, delta, dq_far = call(
        far_kernel,
        [q, keep0, from_core, from_y, att, kv, probs, factors],
        [block, block, block, shape((ROWS, HD), BF), row_shape, dq_shape],
        [],
        5 * 1024 * 2560 * 128,
        B_MIB,
        doc_lengths,
    )

    got = swap(send, "c")
    run = along_z(add(keep, got).astype(BF), 7, 1)
    q, got = tie(q, got)
    dq, keep2, keep1, send2, send1 = call(
        near_kernel,
        [q, do, delta, kv, probs, factors, dq_far, fifth],
        [shape((128, 1024), BF), block, block, block, block],
        [pltpu.VMEM((HD, ROWS), F32)],
        5 * 1024 * 2560 * 128,
        B_MIB,
        doc_lengths,
    )
    middle = add(keep2, swap(send2, "c"))
    send1, run = tie(send1, run)
    final = add(keep1, swap(send1, "c"))
    run = along_z((run.astype(F32) + middle).astype(BF), 7, 2)
    run = jnp.where(first, run.astype(F32) + final, run.astype(F32)).astype(BF)
    run = along_z(run, 7, 1)
    run = jnp.where(first, run.astype(F32), run.astype(F32) + final)
    total = jnp.where(first, run[:256], run[256:]) + swap(
        jnp.where(first, run[256:], run[:256]).astype(BF), "c"
    ).astype(F32)
    there = swap(jnp.where(yl == 0, total[128:], total[:128]).astype(BF), "yl")
    kv_grad = (jnp.where(yl == 0, total[:128], total[128:]) + there.astype(F32)).astype(BF)
    return (
        dq.reshape(128, 8, HD),
        kv_grad[:, :HD].reshape(128, 1, HD),
        kv_grad[:, HD:].reshape(128, 1, HD),
    )


def solution(mesh):
    grid = Mesh(mesh.devices.reshape(8, 2, 2, 4, 2), ("z", "yl", "c", "x", "yh"))
    ctx, tp = ("z", "yl", "c"), ("x", "yh")
    return jax.shard_map(
        local,
        mesh=grid,
        in_specs=(
            P(ctx, tp, None),
            P(ctx, tp, None),
            P(ctx, tp, None),
            P(ctx + tp, None),
            P(ctx, tp),
            P(),
        ),
        out_specs=(P(ctx, tp, None), P(ctx, tp, None), P(ctx, tp, None)),
        check_vma=False,
    )
```

```python
import math

import jax
import jax.numpy as jnp
from jax import lax
from jax.experimental import pallas as pl
from jax.experimental.pallas import tpu as pltpu
from jax.sharding import Mesh, PartitionSpec as P

BF = jnp.bfloat16
F32 = jnp.float32
NEG = -1e30
HD = 128
SCALE = HD**-0.5
C2 = SCALE * math.log2(math.e)
PLANE = 512
PLANES = 6
ROWS = 1024
MIB = 1024 * 1024
P_MIB, F_MIB, B_MIB = 16, 20, 24
HINT = 0

NT = (((1,), (1,)), ((), ()))
NN = (((1,), (0,)), ((), ()))
TN = (((0,), (0,)), ((), ()))


def dot(a, b, dims):
    return lax.dot_general(a, b, dims, preferred_element_type=F32)


def key_positions(z, d):
    r = lax.broadcasted_iota(jnp.int32, (PLANE, 1), 0)
    part = r >> 7
    block = ((part & 1) << 1) | (part >> 1)
    return (z - d) * PLANE + block * 128 + (r & 127)


def where_am_i():
    z, c = lax.axis_index("z"), lax.axis_index("c")
    return z, c, ((z * 2 + lax.axis_index("yl")) * 2 + c) * 128


def documents(lengths, pos0):
    row_pos = pos0 + (lax.broadcasted_iota(jnp.int32, (1, ROWS), 1) & 127)
    start, low, high = jnp.zeros((1, ROWS), jnp.int32), 0, 0
    end = lengths[0]
    for i in range(8):
        start = jnp.where(end <= row_pos, end, start)
        low = jnp.where(end <= pos0, end, low)
        high = jnp.where(end <= pos0 + 127, end, high)
        if i < 7:
            end = end + lengths[i + 1]
    return row_pos, start, low, high


def project_kernel(gh, gu, gd, gu2, gd2, w0, w1, w2, w3, w4, total, rest, a_scr):
    me = lax.axis_index("yl") * 2 + lax.axis_index("c")
    x, yh = lax.axis_index("x"), lax.axis_index("yh")
    for rel in range(4):
        src = pl.multiple_of((me ^ rel) * 16, 16)
        for half in range(2):
            base = pl.multiple_of(src + half * 64, 16)
            for turn_by, ref, at in (
                (0, gh, base),
                (1, gd, base),
                (2, (gu2, gd2)[half], src),
                (3, gu, base),
            ):
                tp = ((x + turn_by) & 3) * 2 + (yh ^ half)
                row = pl.multiple_of(rel * 128 + tp * 16, 16)
                a_scr[pl.ds(row, 16), :] = ref[pl.ds(at, 16), 0:1280]
                rest[pl.ds(row, 16), :] = ref[pl.ds(at, 16), 1280:2048]
    out = None
    for k, w in enumerate((w0, w1, w2, w3, w4)):
        part = dot(a_scr[:, k * 256 : k * 256 + 256], w[...], NN)
        out = part if out is None else out + part
    total[...] = out


def forward_planes(lengths, q, kv, probs, tops, att, m_row, l_row):
    z, c, pos0 = where_am_i()
    row_pos, start, low, high = documents(lengths, pos0)

    def work(d, masked):
        k = kv[d, :, 0:HD]
        v_t = kv[d, :, HD : 2 * HD].T
        s = dot(k, q[...], NT)
        if masked:
            s = jnp.where(allowed(z, d, row_pos, start), s, NEG)
        old = m_row[...]
        new = jnp.maximum(old, jnp.max(s, axis=0, keepdims=True) * C2)
        shrink = jnp.exp2(old - new)
        p = jnp.exp2(s * C2 - new)
        l_row[...] = l_row[...] * shrink + jnp.sum(p, axis=0, keepdims=True)
        m_row[...] = new
        tops[d] = new
        p = p.astype(BF)
        probs[d] = p
        att[...] = att[...] * shrink + dot(v_t, p, NN)

    each_plane(work, z, 0, z - low // PLANE + 1, high)


def place(kv, i, ref):
    for b in range(4):
        kv[i, b * 128 : b * 128 + 128, :] = ref[:, b * 256 : b * 256 + 256]


def forward_kernel(
    lengths, q, plane, r1, r2, r3, t1, t2, t3, att, kv, probs, factors, m_row, l_row
):
    place(kv, 0, plane)

    @pl.when(lax.axis_index("c") == 0)
    def _():
        for i, ref in enumerate((r1, r2, r3, t2, t1)):
            place(kv, i + 1, ref)

    @pl.when(lax.axis_index("c") != 0)
    def _():
        for i, ref in enumerate((t1, t2, t3, r2, r1)):
            place(kv, i + 1, ref)

    m_row[...] = jnp.full((1, ROWS), NEG, F32)
    l_row[...] = jnp.zeros((1, ROWS), F32)
    att[...] = jnp.zeros((HD, ROWS), F32)
    factors[...] = jnp.zeros((PLANES, 1, ROWS), F32)
    forward_planes(lengths, q, kv, probs, factors, att, m_row, l_row)
    lse = m_row[...] + jnp.log2(l_row[...])
    for i in range(PLANES):
        factors[i] = jnp.exp2(jnp.minimum(factors[i] - lse, 0.0))
    att[...] = att[...] / l_row[...]


def allowed(z, d, row_pos, start):
    keys = key_positions(z, d)
    return (keys >= start) & (keys <= row_pos)


def each_plane(work, z, begin, end, clear):
    def plane(d, carry):
        whole = (d > 0) & ((z - d) * PLANE >= clear)

        @pl.when(whole)
        def _():
            work(d, False)

        @pl.when(jnp.logical_not(whole))
        def _():
            work(d, True)

        return carry

    lax.fori_loop(begin, end, plane, 0)


def gradients(lengths, q, do, kv, probs, factors, delta, dq_t, begin, store):
    z, c, pos0 = where_am_i()
    row_pos, start, low, high = documents(lengths, pos0)

    def plane(d, carry):
        k = kv[d, :, 0:HD]
        v = kv[d, :, HD : 2 * HD]
        k_t = k.T
        p = probs[d].astype(F32) * factors[d]
        dv = dot(p.astype(BF), do[...], NN)
        dp = dot(v, do[...], NT)
        ds = (p * (dp - delta[...])).astype(BF)
        dk = dot(ds, q[...], NN) * SCALE
        dq_t[...] += dot(k_t, ds, NN)
        store(d, jnp.concatenate([dk, dv], axis=1).astype(BF))
        return carry

    stop = jnp.clip(z - low // PLANE + 1, begin, begin + 3)
    lax.fori_loop(begin, stop, plane, 0)

    def blank(d, carry):
        store(d, jnp.zeros((PLANE, 2 * HD), BF))
        return carry

    lax.fori_loop(stop, begin + 3, blank, 0)


def far_kernel(
    lengths, q, o0, o1, o2, att, kv, probs, factors, keep, send, fifth, do, delta, dq_t
):
    c = lax.axis_index("c")
    o = (o0[...] + o1[...].astype(F32) + o2[...].astype(F32)).astype(BF)
    for h in range(8):
        cols = slice(h * 128, h * 128 + 128)
        do[cols, :] = o[:, cols]
        delta[:, cols] = jnp.sum(o[:, cols].astype(F32).T * att[:, cols], axis=0, keepdims=True)
    dq_t[...] = jnp.zeros((HD, ROWS), F32)

    def store(d, value):
        mine = ((d == 3) & (c == 0)) | ((d == 4) & (c != 0))

        @pl.when(mine)
        def _():
            keep[...] = value

        @pl.when((d < 5) & jnp.logical_not(mine))
        def _():
            send[...] = value

        @pl.when(d == 5)
        def _():
            fifth[...] = value

    gradients(lengths, q, do, kv, probs, factors, delta, dq_t, 3, store)


def near_kernel(
    lengths, q, do, delta, kv, probs, factors, dq_far, fifth, dq, keep2, keep1, send2, send1, dq_t
):
    c = lax.axis_index("c")
    dq_t[...] = dq_far[...]

    @pl.when(c == 0)
    def _():
        send2[...] = fifth[...]

    @pl.when(c != 0)
    def _():
        keep2[...] = fifth[...]

    def store(d, value):
        @pl.when((d == 2) & (c == 0))
        def _():
            keep2[...] = value

        @pl.when((d == 2) & (c != 0))
        def _():
            send2[...] = value

        mine = ((d == 1) & (c == 0)) | ((d == 0) & (c != 0))

        @pl.when(mine)
        def _():
            keep1[...] = value

        @pl.when((d < 2) & jnp.logical_not(mine))
        def _():
            send1[...] = value

    gradients(lengths, q, do, kv, probs, factors, delta, dq_t, 0, store)
    for h in range(8):
        cols = slice(h * 128, h * 128 + 128)
        dq[:, cols] = (dq_t[:, cols] * SCALE).T.astype(BF)


def call(kernel, args, outs, scratch, flops, vmem_mib, scalars=None):
    vmem = pl.BlockSpec(memory_space=pltpu.VMEM)
    first = [] if scalars is None else [pl.BlockSpec(memory_space=pltpu.SMEM)]
    return pl.pallas_call(
        kernel,
        out_shape=outs,
        in_specs=first + [vmem] * len(args),
        out_specs=[vmem] * len(outs),
        scratch_shapes=scratch,
        compiler_params=pltpu.CompilerParams(vmem_limit_bytes=vmem_mib * MIB),
        cost_estimate=pl.CostEstimate(flops=flops, bytes_accessed=6 << 20, transcendentals=0),
    )(*([] if scalars is None else [scalars]), *args)


def tie(*xs):
    return lax.optimization_barrier(xs)


def shape(dims, dtype):
    return jax.ShapeDtypeStruct(dims, dtype)


def swap(x, axis):
    return lax.ppermute(x, axis, [(0, 1), (1, 0)])


def turn(x, step):
    return lax.ppermute(x, "x", [(i, (i + step) % 4) for i in range(4)])


def along_z(x, step0, step1):
    pairs = [(2 * z, 2 * ((z + step0) % 8)) for z in range(8)]
    if step1 is not None:
        pairs += [(2 * z + 1, 2 * ((z + step1) % 8) + 1) for z in range(8)]
    return lax.ppermute(x, ("z", "c"), pairs)


def add(a, b):
    return a.astype(F32) + b.astype(F32)


def local(queries, key_states, value_vectors, grad_output, out_weight, doc_lengths):
    z, yl, c = lax.axis_index("z"), lax.axis_index("yl"), lax.axis_index("c")
    first = c == 0

    rolled = lax.dynamic_slice(
        jnp.concatenate([grad_output, grad_output], axis=1), (0, z * 1024), (16, 8192)
    )

    def columns(to_yl, to_c):
        order = [(0, to_c)]
        for s in (1, 2, 3):
            far = s if to_c else 8 - s
            order += [(far, to_c), (far, 1 - to_c)]
        order.append((4, to_c))
        return jnp.concatenate(
            [rolled[:, s * 1024 + to_yl * 512 + par * 256 :][:, :256] for s, par in order], axis=1
        )

    sent = jnp.stack([columns(a, b) for a in (0, 1) for b in (0, 1)])

    t = swap(jnp.where(first, sent[1::2], sent[0::2]).reshape(32, 2048), "c")
    own = jnp.where(first, sent[0::2], sent[1::2]).reshape(32, 2048)
    both = jnp.where(first, jnp.stack([own, t]), jnp.stack([t, own])).reshape(2, 2, 16, 2048)
    q0 = swap(out_weight, "c")
    both, q0 = tie(both, q0)
    away = swap(jnp.where(yl == 0, both[:, 1], both[:, 0]), "yl")
    here = jnp.where(yl == 0, both[:, 0], both[:, 1])
    got = jnp.where(yl == 0, jnp.stack([here, away]), jnp.stack([away, here])).reshape(64, 2048)
    gh = jnp.concatenate([got, swap(got, "yh")])
    gu, gd = turn(gh, 1), turn(gh, 3)
    gu2, gd2 = turn(gu[:64], 1), turn(gd[64:], 3)

    p1 = along_z(out_weight, 1, 7)
    kv = jnp.concatenate([key_states.reshape(128, HD), value_vectors.reshape(128, HD)], axis=1)
    other = swap(kv, "yl")
    half = jnp.where(
        yl == 0, jnp.concatenate([kv, other], axis=1), jnp.concatenate([other, kv], axis=1)
    )
    other = swap(half, "c")
    plane = jnp.where(
        first, jnp.concatenate([half, other], axis=1), jnp.concatenate([other, half], axis=1)
    )
    q1 = along_z(q0, 1, 7)
    r1 = along_z(plane, 1, 5)
    p2 = along_z(p1, 1, 7)
    q2 = along_z(q1, 1, 7)
    r2 = along_z(tie(r1, q1, p2)[0], 1, 7)
    p3 = along_z(p2, 1, 7)
    q3 = along_z(q2, 1, 7)
    r3 = along_z(r2, 1, None)
    p4 = along_z(p3, 1, 7)

    t1, t2, t3 = swap(r1, "c"), swap(r2, "c"), swap(r3, "c")

    total, rest = call(
        project_kernel,
        [gh, gu, gd, gu2, gd2, out_weight, p1, q1, p2, q2],
        [shape((512, 1024), F32), shape((512, 768), BF)],
        [pltpu.VMEM((512, 1280), BF)],
        HINT * 2 * 512 * 1280 * 1024,
        P_MIB,
    )
    for k, w in enumerate((p3, q3, p4)):
        total = total + dot(rest[:, k * 256 : k * 256 + 256], w, NN)
    total = total.reshape(2, 2, 128, 1024)
    keep0, keep1 = total[0, 0], total[1, 0]
    send, t3 = tie(total[1, 1].astype(BF), t3)
    from_both = swap(send, "c")
    from_core = swap(total[0, 1].astype(BF), "c")
    from_y = swap(add(keep1, from_both).astype(BF), "yl")

    q = queries.transpose(1, 0, 2).reshape(ROWS, HD)
    q, from_both = tie(q, from_both)
    row_shape, dq_shape = shape((1, ROWS), F32), shape((HD, ROWS), F32)
    att, kv, probs, factors = call(
        forward_kernel,
        [q, plane, r1, r2, r3, t1, t2, t3],
        [
            dq_shape,
            shape((PLANES, PLANE, 2 * HD), BF),
            shape((PLANES, PLANE, ROWS), BF),
            shape((PLANES, 1, ROWS), F32),
        ],
        [pltpu.VMEM((1, ROWS), F32)] * 2,
        1,
        F_MIB,
        doc_lengths,
    )

    block = shape((PLANE, 2 * HD), BF)
    keep, send, fifth, do, delta, dq_far = call(
        far_kernel,
        [q, keep0, from_core, from_y, att, kv, probs, factors],
        [block, block, block, shape((ROWS, HD), BF), row_shape, dq_shape],
        [],
        5 * 1024 * 2560 * 128,
        B_MIB,
        doc_lengths,
    )

    got = swap(send, "c")
    run = along_z(add(keep, got).astype(BF), 7, 1)
    q, got = tie(q, got)
    dq, keep2, keep1, send2, send1 = call(
        near_kernel,
        [q, do, delta, kv, probs, factors, dq_far, fifth],
        [shape((128, 1024), BF), block, block, block, block],
        [pltpu.VMEM((HD, ROWS), F32)],
        5 * 1024 * 2560 * 128,
        B_MIB,
        doc_lengths,
    )
    middle = add(keep2, swap(send2, "c"))
    send1, run = tie(send1, run)
    final = add(keep1, swap(send1, "c"))
    run = along_z((run.astype(F32) + middle).astype(BF), 7, 2)
    run = jnp.where(first, run.astype(F32) + final, run.astype(F32)).astype(BF)
    run = along_z(run, 7, 1)
    run = jnp.where(first, run.astype(F32), run.astype(F32) + final)
    total = jnp.where(first, run[:256], run[256:]) + swap(
        jnp.where(first, run[256:], run[:256]).astype(BF), "c"
    ).astype(F32)
    there = swap(jnp.where(yl == 0, total[128:], total[:128]).astype(BF), "yl")
    kv_grad = (jnp.where(yl == 0, total[:128], total[128:]) + there.astype(F32)).astype(BF)
    return (
        dq.reshape(128, 8, HD),
        kv_grad[:, :HD].reshape(128, 1, HD),
        kv_grad[:, HD:].reshape(128, 1, HD),
    )


def solution(mesh):
    grid = Mesh(mesh.devices.reshape(8, 2, 2, 4, 2), ("z", "yl", "c", "x", "yh"))
    ctx, tp = ("z", "yl", "c"), ("x", "yh")
    return jax.shard_map(
        local,
        mesh=grid,
        in_specs=(
            P(ctx, tp, None),
            P(ctx, tp, None),
            P(ctx, tp, None),
            P(ctx + tp, None),
            P(ctx, tp),
            P(),
        ),
        out_specs=(P(ctx, tp, None), P(ctx, tp, None), P(ctx, tp, None)),
        check_vma=False,
    )
```
